512 devices in a mesh: pipe: 8 (over y, core), expert: 64 (over z, x).
Axes of the slice: x: 4, y: 4, z: 16, core: 2. Of those that a mesh axis runs over, the one named last changes fastest.
Arguments:
- upstream: bfloat16 [8, 4096, 2048], P('pipe', 'expert'), may hold values from -6 to 6
- expert_ids: int32 [8, 4096, 8], P('pipe', 'expert'), may hold values from 0 to 63, all different within a row; in each aligned block of 64 rows (0 to 63, 64 to 127, ..., all dimensions but the last counted through in order) at most 16 rows name the same one
- gate_weights: bfloat16 [8, 4096, 8], P('pipe', 'expert'), may hold values from 0.099609375 to 2
- expert_weight: bfloat16 [8, 64, 768, 2048], P('pipe', 'expert'), may hold values from -0.125 to 0.125
Outputs:
- hidden_grad: bfloat16 [8, 4096, 8, 768], P('pipe', 'expert')
The draws below stay inside these ranges and needn't reach their ends.
Inputs may be any that keep to these rules, and one draw needn't show every extreme that they name: `expert_ids`: each token names 8 different experts. Among the 64 tokens of one device (aligned blocks of the section's tokens) no expert is named by more than 16 tokens, and in some blocks one expert is named by exactly 16.
All inputs are finite; a program needn't handle non-finite values.
Results may differ from the reference program's by a relative error of at most 0.001.
Values may be sent and summed in bfloat16 or wider, within the bound.
A program may use at most 64 MiB of HBM per device.

```python
import math
import jax
import jax.numpy as jnp
import numpy as np
from jax import lax

D = 2048
HID = 768
TOPK = 8
TOK_DEV = 64
SECTIONS = 8
EXPERTS = 64
TOKENS = 4096
MOST = 16
N_EXPERT = 64


def block_scale(stream_key, dims, pieces, low, top_value):
    def one(dim, blocks):
        heights = jax.random.uniform(jax.random.fold_in(jax.random.fold_in(stream_key, 6), dim), (blocks,), jnp.float32, low / len(pieces), top_value / len(pieces))
        return jnp.repeat(jnp.exp(heights), dims[dim] // blocks).reshape((-1,) + (1,) * (len(dims) - dim - 1))

    factor_of = one(*pieces[0])
    for cut in pieces[1:]:
        factor_of = factor_of * one(*cut)
    return factor_of


def shared_out(rng, own, number, rows, amount, top, limit, skew):
    sequence = jax.random.permutation(rng, amount)
    packed, common = shares(amount, rows * top, limit, skew, True), shares(amount, rows * top, limit, skew, False)
    places = jnp.arange(amount)

    def named(lengths, rotation):
        used = int((lengths > 0).sum())
        fixed = max(1, used // 4)
        shifted = fixed + (places - fixed + rotation * (used - fixed)) % max(1, amount - fixed)
        return jnp.zeros((amount,), jnp.int32).at[sequence[jnp.where(places < fixed, places, shifted)]].set(jnp.asarray(lengths, jnp.int32))

    lengths = jnp.where(number % 4 == 0, named(packed, number // 4), named(common, number - number // 4 - 1))
    mixed = jax.random.permutation(jax.random.fold_in(own, 3), amount)
    giver, sink = mixed[0:amount // 2 * 2:2], mixed[1:amount // 2 * 2:2]
    slack = jnp.minimum(lengths[giver] - 1, limit - lengths[sink]) // 2
    slack = jnp.where((giver == sequence[0]) | (sink == sequence[0]) | (lengths[sink] == 0), 0, jnp.maximum(slack, 0))
    shifted = jax.random.randint(jax.random.fold_in(own, 4), (amount // 2,), 0, 1 << 20) % (slack + 1)
    lengths = lengths.at[giver].add(-shifted).at[sink].add(shifted)
    labels = jnp.searchsorted(jnp.cumsum(lengths), jnp.arange(rows * top), side="right").astype(jnp.int32)
    grid = labels.reshape(top, rows).T
    grid = grid[jax.random.permutation(jax.random.fold_in(own, 1), rows)]
    rotation = jax.random.randint(jax.random.fold_in(own, 2), (rows, 1), 0, top)
    return jnp.take_along_axis(grid, (jnp.arange(top)[None, :] + rotation) % top, axis=1)


def shares(amount, total, most, lean, full):
    weights = [(1 << 20) // math.isqrt(rank ** lean) + 1 for rank in range(1, amount + 1)]
    largest = most if full else min(most, max(-(-total // amount), total * weights[0] // sum(weights)))
    least = 1 if total - largest >= amount - 1 else 0
    counts, rest = [largest] + [least] * (amount - 1), total - largest - least * (amount - 1)
    while rest > 0:
        free = [i for i in range(1, amount) if counts[i] < largest] or [i for i in range(1, amount) if counts[i] < most]
        mass, budget = sum([weights[i] for i in free]), rest
        for i in free:
            more = min(most - counts[i], max(1, budget * weights[i] // mass), rest)
            counts[i] = counts[i] + more
            rest = rest - more
    return np.array(counts)


def centred(key, shape, spread, reach, shards=(), kind=jnp.bfloat16):
    result = spread * jax.random.normal(key, shape, jnp.float32)
    if shards:
        result = result * block_scale(key, shape, shards, -0.22, 0.18)
    return jnp.clip(result, -reach, reach).astype(kind)


def setup_inputs(seed: int = 0) -> dict:
    key_of = jax.random.split(jax.random.key(seed), 5)
    upstream = centred(key_of[0], (SECTIONS, TOKENS, D), 1.0, 6.0, ((0, 8), (1, 64)))
    expert_ids_keys = jax.random.split(jax.random.fold_in(key_of[1], 1), SECTIONS * TOKENS // TOK_DEV)
    expert_ids_turns = jax.random.permutation(jax.random.fold_in(key_of[1], 3), SECTIONS * TOKENS // TOK_DEV)
    expert_ids = jax.vmap(lambda own, number: shared_out(jax.random.fold_in(key_of[1], 2), own, number, TOK_DEV, EXPERTS, TOPK, MOST, 2))(expert_ids_keys, expert_ids_turns).reshape((SECTIONS, TOKENS, TOPK))
    gate_weights = jnp.clip(jnp.exp(math.log(2.0) - 2.9996462 * jax.random.uniform(key_of[2], (SECTIONS, TOKENS, TOPK), jnp.float32) ** block_scale(key_of[2], (SECTIONS, TOKENS, TOPK), ((0, 8), (1, 64)), -0.2, 0.2)), 0.099609375, 2.0).astype(jnp.bfloat16)
    expert_weight = centred(key_of[3], (SECTIONS, EXPERTS, HID, D), D ** -0.5, 0.125, ((0, 8), (1, 64)))
    return {"upstream": upstream, "expert_ids": expert_ids, "gate_weights": gate_weights, "expert_weight": expert_weight}


def route_ranks(flat_routes):
    owners = jnp.arange(EXPERTS, dtype=jnp.int32)
    matched = (flat_routes[:, None] == owners[None, :]).astype(jnp.int32)
    before = (jnp.cumsum(matched, axis=0) - matched).astype(jnp.int32)
    return jnp.sum(before * matched, axis=1).astype(jnp.int32)


def reference(upstream, expert_ids, gate_weights, expert_weight):
    section_grads = jnp.roll(upstream, -1, axis=0)
    capacity = N_EXPERT * MOST
    route_count = TOKENS * TOPK

    def one_section(inputs):
        token_grads, section_ids, section_gates, section_weights = inputs
        flat_routes = section_ids.reshape(route_count).astype(jnp.int32)
        slot_rank = route_ranks(flat_routes)
        route_index = jnp.arange(route_count, dtype=jnp.int32)
        slot_table = jnp.zeros((EXPERTS, capacity), jnp.int32).at[flat_routes, slot_rank].set(route_index)

        def one_expert(expert_pair):
            slot_routes, weight_mat = expert_pair
            token_index = (slot_routes // TOPK).astype(jnp.int32)
            slot_rows = jnp.take(token_grads, token_index, axis=0).astype(jnp.float32)
            return jnp.dot(slot_rows, weight_mat.astype(jnp.float32).T, precision=lax.Precision.HIGHEST)

        products = lax.map(one_expert, (slot_table, section_weights))
        route_prod = products[flat_routes, slot_rank]
        scaled = section_gates.reshape(route_count, 1).astype(jnp.float32) * route_prod
        return scaled.astype(jnp.bfloat16).reshape(TOKENS, TOPK, HID)

    return lax.map(one_section, (section_grads, expert_ids, gate_weights, expert_weight))
```

```python
import functools

import jax
import jax.numpy as jnp
from jax import lax
from jax.experimental import pallas as pl
from jax.experimental.pallas import tpu as pltpu
from jax.sharding import PartitionSpec as P

MESH = pl.DeviceIdType.MESH
NX = 4
MOST = 16
LANES = 128
HALF = 64


def iota(shape, dim):
    return lax.broadcasted_iota(jnp.int32, shape, dim)


def kernel(
    pipes,
    experts,
    up_ref,
    ids_ref,
    gates_ref,
    w_hbm,
    out_ref,
    tok,
    table,
    own_table,
    sel,
    rows_in,
    prod,
    ret,
    acc,
    pos,
    w_ref,
    local_sem,
    ring_send,
    ring_recv,
    table_send,
    table_recv,
    shift_sem,
    sel_send,
    sel_recv,
    ret_send,
    ret_recv,
):
    nz = experts // NX
    steps = nz // 2
    tokens, width = up_ref.shape
    topk = ids_ref.shape[0]
    hidden = w_hbm.shape[0]
    p = lax.axis_index("pipe")
    e = lax.axis_index("expert")
    z = e // NX
    x = e % NX
    after = (p + 1) % pipes
    before = (p + pipes - 1) % pipes

    def at(zz, xx):
        return ((zz + nz) % nz) * NX + xx

    barrier = pltpu.get_barrier_semaphore()

    def greet(d, carry):
        pl.semaphore_signal(barrier, inc=1, device_id=(p, (e + d) % experts), device_id_type=MESH)
        return carry

    lax.fori_loop(1, experts, greet, 0)
    for xx in range(NX):
        pl.semaphore_signal(barrier, inc=1, device_id=(after, at(z, xx)), device_id_type=MESH)
    pl.semaphore_signal(barrier, inc=1, device_id=(before, e), device_id_type=MESH)
    pl.semaphore_wait(barrier, experts - 1 + NX + 1)

    def ring(direction, hop, src):
        dst = hop if direction == 0 else nz - hop
        return pltpu.make_async_remote_copy(
            src_ref=src,
            dst_ref=tok.at[dst],
            send_sem=ring_send.at[direction, hop],
            recv_sem=ring_recv.at[direction, hop],
            device_id=(p, at(z + 1 - 2 * direction, x)),
            device_id_type=MESH,
        )

    def ring_table(direction, hop, src):
        dst = hop if direction == 0 else nz - hop
        return pltpu.make_async_remote_copy(
            src_ref=src,
            dst_ref=table.at[dst],
            send_sem=table_send.at[direction, hop],
            recv_sem=table_recv.at[direction, hop],
            device_id=(p, at(z + 1 - 2 * direction, x)),
            device_id_type=MESH,
        )

    ring(0, 1, up_ref).start()
    ring(1, 1, up_ref).start()
    own_copy = pltpu.make_async_copy(up_ref, tok.at[0], local_sem.at[0])
    own_copy.start()
    w_copy = pltpu.make_async_copy(w_hbm, w_ref, local_sem.at[1])
    w_copy.start()

    packed = jnp.concatenate(
        [ids_ref[...].astype(jnp.float32), gates_ref[...].astype(jnp.float32)], axis=0
    ).astype(jnp.bfloat16)
    eye = (iota((tokens, tokens), 0) == iota((tokens, tokens), 1)).astype(jnp.bfloat16)
    columns = lax.dot_general(
        eye, packed, (((1,), (1,)), ((), ())), preferred_element_type=jnp.float32
    )
    lane = iota((tokens, LANES), 1)
    lane_expert = (lane % HALF).astype(jnp.float32)
    named = jnp.zeros((tokens, LANES), jnp.float32)
    gate = jnp.zeros((tokens, LANES), jnp.float32)
    for k in range(topk):
        hit = columns[:, k : k + 1] == lane_expert
        named = jnp.where(hit, 1.0, named)
        gate = jnp.where(hit, columns[:, topk + k : topk + k + 1], gate)
    lower = (iota((tokens, tokens), 1) < iota((tokens, tokens), 0)).astype(jnp.bfloat16)
    rank = jnp.dot(lower, named.astype(jnp.bfloat16), preferred_element_type=jnp.float32)
    value = jnp.where(lane < HALF, (iota((tokens, LANES), 0) + 1).astype(jnp.float32), gate)
    value = jnp.where(named > 0.5, value, 0.0)
    table_rows = [
        jnp.sum(jnp.where(rank == float(r), value, 0.0), axis=0, keepdims=True)
        for r in range(MOST)
    ]
    own_table[...] = jnp.concatenate(table_rows, axis=0).astype(jnp.bfloat16)

    shift = pltpu.make_async_remote_copy(
        src_ref=own_table,
        dst_ref=table.at[0],
        send_sem=shift_sem.at[0],
        recv_sem=shift_sem.at[1],
        device_id=(after, e),
        device_id_type=MESH,
    )
    shift.start()

    ranks = []
    for k in range(topk):
        hit = (columns[:, k : k + 1] == lane_expert) & (lane < HALF)
        ranks.append(jnp.sum(jnp.where(hit, rank, 0.0), axis=1, keepdims=True))
    lane8 = iota((tokens, 2 * topk), 1)
    both = jnp.where(lane8 < topk, columns, 0.0)
    for k in range(topk):
        both = jnp.where(lane8 == topk + k, ranks[k], both)
    routes = tokens * topk
    spread = (iota((routes, tokens), 0) // topk == iota((routes, tokens), 1)).astype(jnp.bfloat16)
    by_route = jnp.dot(spread, both.astype(jnp.bfloat16), preferred_element_type=jnp.float32)
    which = iota((routes, 2 * topk), 0) % topk
    lane_r = iota((routes, 2 * topk), 1)
    slot = jnp.sum(
        jnp.where(lane_r == which, by_route * MOST, 0.0)
        + jnp.where(lane_r == which + topk, by_route, 0.0),
        axis=1,
        keepdims=True,
    )
    slot = slot - (z * (NX * MOST)).astype(jnp.float32)
    slot = jnp.where(slot < 0.0, slot + float(experts * MOST), slot)
    pos[...] = jnp.broadcast_to(slot, (routes, LANES))

    shift.wait()
    ring_table(0, 1, table.at[0]).start()
    ring_table(1, 1, table.at[0]).start()
    w_copy.wait()

    def pair(i):
        return i % steps, nz - i

    def sel_copy(i, xx):
        return pltpu.make_async_remote_copy(
            src_ref=sel.at[i - 1, xx],
            dst_ref=rows_in.at[i - 1, x],
            send_sem=sel_send.at[i - 1, xx],
            recv_sem=sel_recv.at[i - 1, x],
            device_id=(before, at(z, xx)),
            device_id_type=MESH,
        )

    def choose(i):
        table_lane = iota((MOST, LANES), 1)
        token_lane = (iota((MOST, tokens), 1) + 1).astype(jnp.float32)
        for half, j in enumerate(pair(i)):
            slots = table[j].astype(jnp.float32)
            picks = []
            for xx in range(NX):
                expert = at(z, xx)
                token = jnp.sum(
                    jnp.where(table_lane == expert, slots, 0.0), axis=1, keepdims=True
                )
                weight = jnp.sum(
                    jnp.where(table_lane == expert + HALF, slots, 0.0), axis=1, keepdims=True
                )
                picks.append((token == token_lane).astype(jnp.bfloat16))
                sel[i - 1, xx, half * MOST : (half + 1) * MOST, width:] = jnp.broadcast_to(
                    weight, (MOST, LANES)
                ).astype(jnp.bfloat16)
            pick = jnp.concatenate(picks, axis=0)
            part = min(512, width)
            for c in range(0, width, part):
                rows = jnp.dot(
                    pick, tok[j, :, c : c + part], preferred_element_type=jnp.float32
                ).astype(jnp.bfloat16)
                for xx in range(NX):
                    sel[i - 1, xx, half * MOST : (half + 1) * MOST, c : c + part] = rows[
                        xx * MOST : (xx + 1) * MOST
                    ]
        for d in range(NX):
            sel_copy(i, (x + d) % NX).start()

    def ret_copy(i, half, j, d, local=False):
        xx = (x + d) % NX
        src = prod.at[i - 1, pl.ds(pl.multiple_of((xx * 2 + half) * MOST, MOST), MOST)]
        dst = ret.at[j, pl.ds(pl.multiple_of(x * MOST, MOST), MOST)]
        if local:
            return pltpu.make_async_copy(src, dst, ret_recv.at[j, x])
        return pltpu.make_async_remote_copy(
            src_ref=src,
            dst_ref=dst,
            send_sem=ret_send.at[i - 1, half, d],
            recv_sem=ret_recv.at[j, x],
            device_id=(p, at(z - j, xx)),
            device_id_type=MESH,
        )

    def multiply(i):
        for d in range(NX):
            xx = (x + d) % NX
            pltpu.make_async_copy(
                rows_in.at[i - 1, xx], rows_in.at[i - 1, xx], sel_recv.at[i - 1, xx]
            ).wait()
        count = NX * 2 * MOST
        gates = rows_in[i - 1, :, :, width:].reshape(count, LANES).astype(jnp.float32)
        for n in range(0, hidden, 256):
            out = lax.dot_general(
                rows_in[i - 1, :, :, :width].reshape(count, width),
                w_ref[n : n + 256],
                (((1,), (1,)), ((), ())),
                preferred_element_type=jnp.float32,
            )
            for c in range(0, 256, LANES):
                prod[i - 1, :, n + c : n + c + LANES] = (
                    out[:, c : c + LANES] * gates
                ).astype(jnp.bfloat16)
        for half, j in enumerate(pair(i)):
            for d in range(NX):
                if half == 0 and d == 0:
                    pl.when(i == steps)(lambda: ret_copy(i, 0, j, 0, local=True).start())
                    pl.when(i < steps)(lambda: ret_copy(i, 0, j, 0).start())
                else:
                    ret_copy(i, half, j, d).start()

    def step(i, carry):
        @pl.when(i < steps)
        def _():
            ring(0, i, up_ref).wait_recv()

        @pl.when(i < steps - 1)
        def _():
            ring(0, i + 1, tok.at[i]).start()

        ring(1, i, up_ref).wait_recv()

        @pl.when(i < steps)
        def _():
            ring(1, i + 1, tok.at[nz - i]).start()
            ring_table(0, i, table.at[0]).wait_recv()

        @pl.when(i < steps - 1)
        def _():
            ring_table(0, i + 1, table.at[i]).start()

        ring_table(1, i, table.at[0]).wait_recv()

        @pl.when(i < steps)
        def _():
            ring_table(1, i + 1, table.at[nz - i]).start()

        @pl.when(i == steps)
        def _():
            own_copy.wait()

        choose(i)

        @pl.when(i >= 2)
        def _():
            multiply(i - 1)

        return carry

    lax.fori_loop(1, steps + 1, step, 0)
    multiply(steps)
    acc[...] = jnp.zeros_like(acc)

    def place(i, carry):
        a, b = pair(i)
        for j in (a, b):
            for xx in range(NX):
                here = ret.at[j, xx * MOST : (xx + 1) * MOST]
                pltpu.make_async_copy(here, here, ret_recv.at[j, xx]).wait()
        span = NX * MOST
        part = min(128, routes)
        lane_q = iota((part, 2 * span), 1)
        want = jnp.where(lane_q < span, a * span + lane_q, (b - 1) * span + lane_q).astype(
            jnp.float32
        )
        rows = jnp.concatenate([ret[a], ret[b]], axis=0)
        for r in range(0, routes, part):
            pick = (pos[r : r + part, : 2 * span] == want).astype(jnp.bfloat16)
            for n in range(0, hidden, 256):
                acc[r : r + part, n : n + 256] += jnp.dot(
                    pick, rows[:, n : n + 256], preferred_element_type=jnp.float32
                )
        return carry

    lax.fori_loop(1, steps + 1, place, 0)
    out_ref[...] = acc[...].astype(jnp.bfloat16)

    def drain(i, carry):
        @pl.when(i < steps)
        def _():
            ring(0, i, up_ref).wait_send()
            ring_table(0, i, table.at[0]).wait_send()

        ring(1, i, up_ref).wait_send()
        ring_table(1, i, table.at[0]).wait_send()
        for xx in range(NX):
            sel_copy(i, xx).wait_send()
        for half, j in enumerate(pair(i)):
            for d in range(NX):
                if half == 0 and d == 0:
                    pl.when(i < steps)(lambda: ret_copy(i, 0, j, 0).wait_send())
                else:
                    ret_copy(i, half, j, d).wait_send()
        return carry

    lax.fori_loop(1, steps + 1, drain, 0)


def per_device(pipes, experts, upstream, expert_ids, gate_weights, expert_weight):
    _, tokens, width = upstream.shape
    topk = expert_ids.shape[2]
    hidden = expert_weight.shape[2]
    nz = experts // NX
    steps = nz // 2
    routes = tokens * topk
    dma = pltpu.SemaphoreType.DMA
    out = pl.pallas_call(
        functools.partial(kernel, pipes, experts),
        out_shape=jax.ShapeDtypeStruct((routes, hidden), jnp.bfloat16),
        in_specs=[
            pl.BlockSpec(memory_space=pl.ANY),
            pl.BlockSpec(memory_space=pltpu.VMEM),
            pl.BlockSpec(memory_space=pltpu.VMEM),
            pl.BlockSpec(memory_space=pl.ANY),
        ],
        out_specs=pl.BlockSpec(memory_space=pltpu.VMEM),
        scratch_shapes=[
            pltpu.VMEM((nz, tokens, width), jnp.bfloat16),
            pltpu.VMEM((nz, MOST, LANES), jnp.bfloat16),
            pltpu.VMEM((MOST, LANES), jnp.bfloat16),
            pltpu.VMEM((steps, NX, 2 * MOST, width + LANES), jnp.bfloat16),
            pltpu.VMEM((steps, NX, 2 * MOST, width + LANES), jnp.bfloat16),
            pltpu.VMEM((steps, NX * 2 * MOST, hidden), jnp.bfloat16),
            pltpu.VMEM((nz, NX * MOST, hidden), jnp.bfloat16),
            pltpu.VMEM((routes, hidden), jnp.float32),
            pltpu.VMEM((routes, LANES), jnp.float32),
            pltpu.VMEM((hidden, width), jnp.bfloat16),
            dma((2,)),
            dma((2, steps + 1)),
            dma((2, steps + 1)),
            dma((2, steps + 1)),
            dma((2, steps + 1)),
            dma((2,)),
            dma((steps, NX)),
            dma((steps, NX)),
            dma((steps, 2, NX)),
            dma((nz, NX)),
        ],
        compiler_params=pltpu.CompilerParams(
            collective_id=0, has_side_effects=True, vmem_limit_bytes=48 * 1024 * 1024
        ),
        cost_estimate=pl.CostEstimate(
            flops=2 * 2 * routes * width * hidden, bytes_accessed=8 << 20, transcendentals=0
        ),
    )(
        upstream[0],
        jnp.swapaxes(expert_ids[0], 0, 1),
        jnp.swapaxes(gate_weights[0], 0, 1),
        expert_weight[0, 0],
    )
    return out.reshape(1, tokens, topk, hidden)


def solution(mesh):
    in_specs = (
        P("pipe", "expert", None),
        P("pipe", "expert", None),
        P("pipe", "expert", None),
        P("pipe", "expert", None, None),
    )
    out_specs = P("pipe", "expert", None, None)
    return jax.shard_map(
        functools.partial(per_device, mesh.shape["pipe"], mesh.shape["expert"]),
        mesh=mesh,
        in_specs=in_specs,
        out_specs=out_specs,
        check_vma=False,
    )
```

```python
import functools

import jax
import jax.numpy as jnp
from jax import lax
from jax.experimental import pallas as pl
from jax.experimental.pallas import tpu as pltpu
from jax.sharding import PartitionSpec as P

MESH = pl.DeviceIdType.MESH
NX = 4
MOST = 16
LANES = 128
HALF = 64
CHUNKS = 2


def iota(shape, dim):
    return lax.broadcasted_iota(jnp.int32, shape, dim)


def kernel(
    pipes,
    experts,
    up_ref,
    ids_hbm,
    gates_hbm,
    w_hbm,
    out_ref,
    tok,
    table,
    own_table,
    sel,
    rows_in,
    prod,
    ret,
    acc,
    pos,
    w_ref,
    ids_ref,
    gates_ref,
    local_sem,
    ring_send,
    ring_recv,
    table_send,
    table_recv,
    shift_sem,
    sel_send,
    sel_recv,
    ret_send,
    ret_recv,
):
    nz = experts // NX
    steps = nz // 2
    tokens, width = up_ref.shape
    topk = ids_hbm.shape[0]
    hidden = w_hbm.shape[0]
    p = lax.axis_index("pipe")
    e = lax.axis_index("expert")
    z = e // NX
    x = e % NX
    after = (p + 1) % pipes
    before = (p + pipes - 1) % pipes

    def at(zz, xx):
        return ((zz + nz) % nz) * NX + xx

    ids_copy = pltpu.make_async_copy(ids_hbm, ids_ref, local_sem.at[2])
    ids_copy.start()
    gates_copy = pltpu.make_async_copy(gates_hbm, gates_ref, local_sem.at[3])
    gates_copy.start()
    own_copy = pltpu.make_async_copy(up_ref, tok.at[0], local_sem.at[0])
    own_copy.start()
    w_copy = pltpu.make_async_copy(w_hbm, w_ref, local_sem.at[1])
    w_copy.start()

    barrier = pltpu.get_barrier_semaphore()

    for other in (at(z + 1, x), at(z - 1, x)):
        pl.semaphore_signal(barrier, inc=1, device_id=(p, other), device_id_type=MESH)
    for xx in range(NX):
        pl.semaphore_signal(barrier, inc=1, device_id=(after, at(z, xx)), device_id_type=MESH)
    pl.semaphore_signal(barrier, inc=1, device_id=(before, e), device_id_type=MESH)
    pl.semaphore_wait(barrier, 2 + NX + 1)

    def ring(direction, hop, src, c):
        dst = hop if direction == 0 else nz - hop
        part = pl.ds(c * (tokens // CHUNKS), tokens // CHUNKS)
        return pltpu.make_async_remote_copy(
            src_ref=src.at[part],
            dst_ref=tok.at[dst, part],
            send_sem=ring_send.at[direction, hop, c],
            recv_sem=ring_recv.at[direction, hop, c],
            device_id=(p, at(z + 1 - 2 * direction, x)),
            device_id_type=MESH,
        )

    def ring_table(direction, hop, src):
        dst = hop if direction == 0 else nz - hop
        return pltpu.make_async_remote_copy(
            src_ref=src,
            dst_ref=table.at[dst],
            send_sem=table_send.at[direction, hop],
            recv_sem=table_recv.at[direction, hop],
            device_id=(p, at(z + 1 - 2 * direction, x)),
            device_id_type=MESH,
        )

    for c in range(CHUNKS):
        for way in range(2):
            ring(way, 1, up_ref, c).start()
    ids_copy.wait()
    gates_copy.wait()

    packed = jnp.concatenate(
        [ids_ref[...].astype(jnp.float32), gates_ref[...].astype(jnp.float32)], axis=0
    ).astype(jnp.bfloat16)
    eye = (iota((tokens, tokens), 0) == iota((tokens, tokens), 1)).astype(jnp.bfloat16)
    columns = lax.dot_general(
        eye, packed, (((1,), (1,)), ((), ())), preferred_element_type=jnp.float32
    )
    lane = iota((tokens, LANES), 1)
    lane_expert = (lane % HALF).astype(jnp.float32)
    named = jnp.zeros((tokens, LANES), jnp.float32)
    gate = jnp.zeros((tokens, LANES), jnp.float32)
    for k in range(topk):
        hit = columns[:, k : k + 1] == lane_expert
        named = jnp.where(hit, 1.0, named)
        gate = jnp.where(hit, columns[:, topk + k : topk + k + 1], gate)
    lower = (iota((tokens, tokens), 1) < iota((tokens, tokens), 0)).astype(jnp.bfloat16)
    rank = jnp.dot(lower, named.astype(jnp.bfloat16), preferred_element_type=jnp.float32)
    value = jnp.where(lane < HALF, (iota((tokens, LANES), 0) + 1).astype(jnp.float32), gate)
    value = jnp.where(named > 0.5, value, 0.0)
    table_rows = [
        jnp.sum(jnp.where(rank == float(r), value, 0.0), axis=0, keepdims=True)
        for r in range(MOST)
    ]
    own_table[...] = jnp.concatenate(table_rows, axis=0).astype(jnp.bfloat16)

    shift = pltpu.make_async_remote_copy(
        src_ref=own_table,
        dst_ref=table.at[0],
        send_sem=shift_sem.at[0],
        recv_sem=shift_sem.at[1],
        device_id=(after, e),
        device_id_type=MESH,
    )
    shift.start()

    ranks = []
    for k in range(topk):
        hit = (columns[:, k : k + 1] == lane_expert) & (lane < HALF)
        ranks.append(jnp.sum(jnp.where(hit, rank, 0.0), axis=1, keepdims=True))
    lane8 = iota((tokens, 2 * topk), 1)
    both = jnp.where(lane8 < topk, columns, 0.0)
    for k in range(topk):
        both = jnp.where(lane8 == topk + k, ranks[k], both)
    routes = tokens * topk
    spread = (iota((routes, tokens), 0) // topk == iota((routes, tokens), 1)).astype(jnp.bfloat16)
    by_route = jnp.dot(spread, both.astype(jnp.bfloat16), preferred_element_type=jnp.float32)
    which = iota((routes, 2 * topk), 0) % topk
    lane_r = iota((routes, 2 * topk), 1)
    slot = jnp.sum(
        jnp.where(lane_r == which, by_route * MOST, 0.0)
        + jnp.where(lane_r == which + topk, by_route, 0.0),
        axis=1,
        keepdims=True,
    )
    slot = slot - (z * (NX * MOST)).astype(jnp.float32)
    slot = jnp.where(slot < 0.0, slot + float(experts * MOST), slot)
    pos[...] = jnp.broadcast_to(slot, (routes, LANES))

    shift.wait()
    ring_table(0, 1, table.at[0]).start()
    ring_table(1, 1, table.at[0]).start()
    w_copy.wait()

    def pair(i):
        return i % steps, nz - i

    def sel_copy(i, xx):
        return pltpu.make_async_remote_copy(
            src_ref=sel.at[i - 1, xx],
            dst_ref=rows_in.at[i - 1, x],
            send_sem=sel_send.at[i - 1, xx],
            recv_sem=sel_recv.at[i - 1, x],
            device_id=(before, at(z, xx)),
            device_id_type=MESH,
        )

    def choose(i):
        table_lane = iota((MOST, LANES), 1)
        token_lane = (iota((MOST, tokens), 1) + 1).astype(jnp.float32)
        for half, j in enumerate(pair(i)):
            slots = table[j].astype(jnp.float32)
            picks = []
            for xx in range(NX):
                expert = at(z, xx)
                token = jnp.sum(
                    jnp.where(table_lane == expert, slots, 0.0), axis=1, keepdims=True
                )
                weight = jnp.sum(
                    jnp.where(table_lane == expert + HALF, slots, 0.0), axis=1, keepdims=True
                )
                picks.append((token == token_lane).astype(jnp.bfloat16))
                sel[i - 1, xx, half * MOST : (half + 1) * MOST, width:] = jnp.broadcast_to(
                    weight, (MOST, LANES)
                ).astype(jnp.bfloat16)
            pick = jnp.concatenate(picks, axis=0)
            part = min(512, width)
            for c in range(0, width, part):
                rows = jnp.dot(
                    pick, tok[j, :, c : c + part], preferred_element_type=jnp.float32
                ).astype(jnp.bfloat16)
                for xx in range(NX):
                    sel[i - 1, xx, half * MOST : (half + 1) * MOST, c : c + part] = rows[
                        xx * MOST : (xx + 1) * MOST
                    ]
        for d in range(NX):
            sel_copy(i, (x + d) % NX).start()

    def ret_copy(i, half, j, d, local=False):
        xx = (x + d) % NX
        src = prod.at[i - 1, pl.ds(pl.multiple_of((xx * 2 + half) * MOST, MOST), MOST)]
        dst = ret.at[j, pl.ds(pl.multiple_of(x * MOST, MOST), MOST)]
        if local:
            return pltpu.make_async_copy(src, dst, ret_recv.at[j, x])
        return pltpu.make_async_remote_copy(
            src_ref=src,
            dst_ref=dst,
            send_sem=ret_send.at[i - 1, half, d],
            recv_sem=ret_recv.at[j, x],
            device_id=(p, at(z - j, xx)),
            device_id_type=MESH,
        )

    def multiply(i):
        for d in range(NX):
            xx = (x + d) % NX
            pltpu.make_async_copy(
                rows_in.at[i - 1, xx], rows_in.at[i - 1, xx], sel_recv.at[i - 1, xx]
            ).wait()
        count = NX * 2 * MOST
        gates = rows_in[i - 1, :, :, width:].reshape(count, LANES).astype(jnp.float32)
        for n in range(0, hidden, 256):
            out = lax.dot_general(
                rows_in[i - 1, :, :, :width].reshape(count, width),
                w_ref[n : n + 256],
                (((1,), (1,)), ((), ())),
                preferred_element_type=jnp.float32,
            )
            for c in range(0, 256, LANES):
                prod[i - 1, :, n + c : n + c + LANES] = (
                    out[:, c : c + LANES] * gates
                ).astype(jnp.bfloat16)
        for half, j in enumerate(pair(i)):
            for d in range(NX):
                if half == 0 and d == 0:
                    pl.when(i == steps)(lambda: ret_copy(i, 0, j, 0, local=True).start())
                    pl.when(i < steps)(lambda: ret_copy(i, 0, j, 0).start())
                else:
                    ret_copy(i, half, j, d).start()

    def step(i, carry):
        for c in range(CHUNKS):
            for way in range(2):
                last = steps - 1 + (c * 2 // CHUNKS == way)

                @pl.when(i <= last)
                def _():
                    ring(way, i, up_ref, c).wait_recv()

                @pl.when(i < last)
                def _():
                    ring(way, i + 1, tok.at[i if way == 0 else nz - i], c).start()

        @pl.when(i < steps)
        def _():
            ring_table(0, i, table.at[0]).wait_recv()

        @pl.when(i < steps - 1)
        def _():
            ring_table(0, i + 1, table.at[i]).start()

        ring_table(1, i, table.at[0]).wait_recv()

        @pl.when(i < steps)
        def _():
            ring_table(1, i + 1, table.at[nz - i]).start()

        @pl.when(i == steps)
        def _():
            own_copy.wait()

        choose(i)

        @pl.when(i >= 2)
        def _():
            multiply(i - 1)

        return carry

    lax.fori_loop(1, steps + 1, step, 0)
    multiply(steps)
    acc[...] = jnp.zeros_like(acc)

    def place(i, carry):
        a, b = pair(i)
        for j in (a, b):
            for xx in range(NX):
                here = ret.at[j, xx * MOST : (xx + 1) * MOST]
                pltpu.make_async_copy(here, here, ret_recv.at[j, xx]).wait()
        span = NX * MOST
        part = min(128, routes)
        lane_q = iota((part, 2 * span), 1)
        want = jnp.where(lane_q < span, a * span + lane_q, (b - 1) * span + lane_q).astype(
            jnp.float32
        )
        rows = jnp.concatenate([ret[a], ret[b]], axis=0)
        for r in range(0, routes, part):
            pick = (pos[r : r + part, : 2 * span] == want).astype(jnp.bfloat16)
            for n in range(0, hidden, 256):
                acc[r : r + part, n : n + 256] += jnp.dot(
                    pick, rows[:, n : n + 256], preferred_element_type=jnp.float32
                )
        return carry

    lax.fori_loop(1, steps + 1, place, 0)
    out_ref[...] = acc[...].astype(jnp.bfloat16)

    def drain(i, carry):
        for c in range(CHUNKS):
            for way in range(2):
                last = steps - 1 + (c * 2 // CHUNKS == way)
                pl.when(i <= last)(lambda: ring(way, i, up_ref, c).wait_send())
        pl.when(i < steps)(lambda: ring_table(0, i, table.at[0]).wait_send())
        ring_table(1, i, table.at[0]).wait_send()
        for xx in range(NX):
            sel_copy(i, xx).wait_send()
        for half, j in enumerate(pair(i)):
            for d in range(NX):
                if half == 0 and d == 0:
                    pl.when(i < steps)(lambda: ret_copy(i, 0, j, 0).wait_send())
                else:
                    ret_copy(i, half, j, d).wait_send()
        return carry

    lax.fori_loop(1, steps + 1, drain, 0)


def per_device(pipes, experts, upstream, expert_ids, gate_weights, expert_weight):
    _, tokens, width = upstream.shape
    topk = expert_ids.shape[2]
    hidden = expert_weight.shape[2]
    nz = experts // NX
    steps = nz // 2
    routes = tokens * topk
    dma = pltpu.SemaphoreType.DMA
    out = pl.pallas_call(
        functools.partial(kernel, pipes, experts),
        out_shape=jax.ShapeDtypeStruct((routes, hidden), jnp.bfloat16),
        in_specs=[
            pl.BlockSpec(memory_space=pltpu.HBM),
            pl.BlockSpec(memory_space=pltpu.HBM),
            pl.BlockSpec(memory_space=pltpu.HBM),
            pl.BlockSpec(memory_space=pltpu.HBM),
        ],
        out_specs=pl.BlockSpec(memory_space=pltpu.VMEM),
        scratch_shapes=[
            pltpu.VMEM((nz, tokens, width), jnp.bfloat16),
            pltpu.VMEM((nz, MOST, LANES), jnp.bfloat16),
            pltpu.VMEM((MOST, LANES), jnp.bfloat16),
            pltpu.VMEM((steps, NX, 2 * MOST, width + LANES), jnp.bfloat16),
            pltpu.VMEM((steps, NX, 2 * MOST, width + LANES), jnp.bfloat16),
            pltpu.VMEM((steps, NX * 2 * MOST, hidden), jnp.bfloat16),
            pltpu.VMEM((nz, NX * MOST, hidden), jnp.bfloat16),
            pltpu.VMEM((routes, hidden), jnp.float32),
            pltpu.VMEM((routes, LANES), jnp.float32),
            pltpu.VMEM((hidden, width), jnp.bfloat16),
            pltpu.VMEM((topk, tokens), jnp.int32),
            pltpu.VMEM((topk, tokens), jnp.bfloat16),
            dma((4,)),
            dma((2, steps + 1, CHUNKS)),
            dma((2, steps + 1, CHUNKS)),
            dma((2, steps + 1)),
            dma((2, steps + 1)),
            dma((2,)),
            dma((steps, NX)),
            dma((steps, NX)),
            dma((steps, 2, NX)),
            dma((nz, NX)),
        ],
        compiler_params=pltpu.CompilerParams(
            collective_id=0, has_side_effects=True, vmem_limit_bytes=62 * 1024 * 1024
        ),
        cost_estimate=pl.CostEstimate(
            flops=2 * 2 * routes * width * hidden, bytes_accessed=8 << 20, transcendentals=0
        ),
    )(
        upstream[0],
        jnp.swapaxes(expert_ids[0], 0, 1),
        jnp.swapaxes(gate_weights[0], 0, 1),
        expert_weight[0, 0],
    )
    return out.reshape(1, tokens, topk, hidden)


def solution(mesh):
    in_specs = (
        P("pipe", "expert", None),
        P("pipe", "expert", None),
        P("pipe", "expert", None),
        P("pipe", "expert", None, None),
    )
    out_specs = P("pipe", "expert", None, None)
    return jax.shard_map(
        functools.partial(per_device, mesh.shape["pipe"], mesh.shape["expert"]),
        mesh=mesh,
        in_specs=in_specs,
        out_specs=out_specs,
        check_vma=False,
    )
```

```python
import functools

import jax
import jax.numpy as jnp
from jax import lax
from jax.experimental import pallas as pl
from jax.experimental.pallas import tpu as pltpu
from jax.sharding import PartitionSpec as P

MESH = pl.DeviceIdType.MESH
NX = 4
MOST = 16
LANES = 128
HALF = 64
CHUNKS = 2


def iota(shape, dim):
    return lax.broadcasted_iota(jnp.int32, shape, dim)


def kernel(
    pipes,
    experts,
    up_ref,
    ids_hbm,
    gates_hbm,
    w_hbm,
    out_ref,
    tok,
    table,
    own_table,
    sel,
    rows_in,
    prod,
    relay,
    ret,
    acc,
    pos,
    w_ref,
    ids_ref,
    gates_ref,
    local_sem,
    ring_send,
    ring_recv,
    table_send,
    table_recv,
    shift_sem,
    sel_send,
    sel_recv,
    ret_send,
    ret_recv,
    leg_send,
    leg_recv,
    last_leg_send,
    last_leg_recv,
    relay_send,
):
    nz = experts // NX
    steps = nz // 2
    tokens, width = up_ref.shape
    topk = ids_hbm.shape[0]
    hidden = w_hbm.shape[0]
    p = lax.axis_index("pipe")
    e = lax.axis_index("expert")
    z = e // NX
    x = e % NX
    after = (p + 1) % pipes
    before = (p + pipes - 1) % pipes

    leg = steps // 2

    def at(zz, xx):
        return ((zz + nz) % nz) * NX + xx

    def slots(xx):
        return pl.ds(pl.multiple_of(xx * MOST, MOST), MOST)

    ids_copy = pltpu.make_async_copy(ids_hbm, ids_ref, local_sem.at[2])
    ids_copy.start()
    gates_copy = pltpu.make_async_copy(gates_hbm, gates_ref, local_sem.at[3])
    gates_copy.start()
    own_copy = pltpu.make_async_copy(up_ref, tok.at[0], local_sem.at[0])
    own_copy.start()
    w_copy = pltpu.make_async_copy(w_hbm, w_ref, local_sem.at[1])
    w_copy.start()

    barrier = pltpu.get_barrier_semaphore()

    for other in (at(z + 1, x), at(z - 1, x)):
        pl.semaphore_signal(barrier, inc=1, device_id=(p, other), device_id_type=MESH)
    for xx in range(NX):
        pl.semaphore_signal(barrier, inc=1, device_id=(after, at(z, xx)), device_id_type=MESH)
    pl.semaphore_signal(barrier, inc=1, device_id=(before, e), device_id_type=MESH)
    pl.semaphore_wait(barrier, 2 + NX + 1)

    def ring(direction, hop, src, c):
        dst = hop if direction == 0 else nz - hop
        part = pl.ds(c * (tokens // CHUNKS), tokens // CHUNKS)
        return pltpu.make_async_remote_copy(
            src_ref=src.at[part],
            dst_ref=tok.at[dst, part],
            send_sem=ring_send.at[direction, hop, c],
            recv_sem=ring_recv.at[direction, hop, c],
            device_id=(p, at(z + 1 - 2 * direction, x)),
            device_id_type=MESH,
        )

    def ring_table(direction, hop, src):
        dst = hop if direction == 0 else nz - hop
        return pltpu.make_async_remote_copy(
            src_ref=src,
            dst_ref=table.at[dst],
            send_sem=table_send.at[direction, hop],
            recv_sem=table_recv.at[direction, hop],
            device_id=(p, at(z + 1 - 2 * direction, x)),
            device_id_type=MESH,
        )

    for c in range(CHUNKS):
        for way in range(2):
            ring(way, 1, up_ref, c).start()
    ids_copy.wait()
    gates_copy.wait()

    packed = jnp.concatenate(
        [ids_ref[...].astype(jnp.float32), gates_ref[...].astype(jnp.float32)], axis=0
    ).astype(jnp.bfloat16)
    eye = (iota((tokens, tokens), 0) == iota((tokens, tokens), 1)).astype(jnp.bfloat16)
    columns = lax.dot_general(
        eye, packed, (((1,), (1,)), ((), ())), preferred_element_type=jnp.float32
    )
    lane = iota((tokens, LANES), 1)
    lane_expert = (lane % HALF).astype(jnp.float32)
    named = jnp.zeros((tokens, LANES), jnp.float32)
    gate = jnp.zeros((tokens, LANES), jnp.float32)
    for k in range(topk):
        hit = columns[:, k : k + 1] == lane_expert
        named = jnp.where(hit, 1.0, named)
        gate = jnp.where(hit, columns[:, topk + k : topk + k + 1], gate)
    lower = (iota((tokens, tokens), 1) < iota((tokens, tokens), 0)).astype(jnp.bfloat16)
    rank = jnp.dot(lower, named.astype(jnp.bfloat16), preferred_element_type=jnp.float32)
    value = jnp.where(lane < HALF, (iota((tokens, LANES), 0) + 1).astype(jnp.float32), gate)
    value = jnp.where(named > 0.5, value, 0.0)
    table_rows = [
        jnp.sum(jnp.where(rank == float(r), value, 0.0), axis=0, keepdims=True)
        for r in range(MOST)
    ]
    own_table[...] = jnp.concatenate(table_rows, axis=0).astype(jnp.bfloat16)

    shift = pltpu.make_async_remote_copy(
        src_ref=own_table,
        dst_ref=table.at[0],
        send_sem=shift_sem.at[0],
        recv_sem=shift_sem.at[1],
        device_id=(after, e),
        device_id_type=MESH,
    )
    shift.start()

    ranks = []
    for k in range(topk):
        hit = (columns[:, k : k + 1] == lane_expert) & (lane < HALF)
        ranks.append(jnp.sum(jnp.where(hit, rank, 0.0), axis=1, keepdims=True))
    lane8 = iota((tokens, 2 * topk), 1)
    both = jnp.where(lane8 < topk, columns, 0.0)
    for k in range(topk):
        both = jnp.where(lane8 == topk + k, ranks[k], both)
    routes = tokens * topk
    spread = (iota((routes, tokens), 0) // topk == iota((routes, tokens), 1)).astype(jnp.bfloat16)
    by_route = jnp.dot(spread, both.astype(jnp.bfloat16), preferred_element_type=jnp.float32)
    which = iota((routes, 2 * topk), 0) % topk
    lane_r = iota((routes, 2 * topk), 1)
    slot = jnp.sum(
        jnp.where(lane_r == which, by_route * MOST, 0.0)
        + jnp.where(lane_r == which + topk, by_route, 0.0),
        axis=1,
        keepdims=True,
    )
    slot = slot - (z * (NX * MOST)).astype(jnp.float32)
    slot = jnp.where(slot < 0.0, slot + float(experts * MOST), slot)
    pos[...] = jnp.broadcast_to(slot, (routes, LANES))

    shift.wait()
    ring_table(0, 1, table.at[0]).start()
    ring_table(1, 1, table.at[0]).start()
    w_copy.wait()

    def pair(i):
        return i % steps, nz - i

    def sel_copy(i, xx):
        return pltpu.make_async_remote_copy(
            src_ref=sel.at[i - 1, xx],
            dst_ref=rows_in.at[i - 1, x],
            send_sem=sel_send.at[i - 1, xx],
            recv_sem=sel_recv.at[i - 1, x],
            device_id=(before, at(z, xx)),
            device_id_type=MESH,
        )

    def choose(i):
        table_lane = iota((MOST, LANES), 1)
        token_lane = (iota((MOST, tokens), 1) + 1).astype(jnp.float32)
        for half, j in enumerate(pair(i)):
            slots = table[j].astype(jnp.float32)
            picks = []
            for xx in range(NX):
                expert = at(z, xx)
                token = jnp.sum(
                    jnp.where(table_lane == expert, slots, 0.0), axis=1, keepdims=True
                )
                weight = jnp.sum(
                    jnp.where(table_lane == expert + HALF, slots, 0.0), axis=1, keepdims=True
                )
                picks.append((token == token_lane).astype(jnp.bfloat16))
                sel[i - 1, xx, half * MOST : (half + 1) * MOST, width:] = jnp.broadcast_to(
                    weight, (MOST, LANES)
                ).astype(jnp.bfloat16)
            pick = jnp.concatenate(picks, axis=0)
            part = min(512, width)
            for c in range(0, width, part):
                rows = jnp.dot(
                    pick, tok[j, :, c : c + part], preferred_element_type=jnp.float32
                ).astype(jnp.bfloat16)
                for xx in range(NX):
                    sel[i - 1, xx, half * MOST : (half + 1) * MOST, c : c + part] = rows[
                        xx * MOST : (xx + 1) * MOST
                    ]
        for d in range(NX):
            sel_copy(i, (x + d) % NX).start()

    def ret_copy(i, half, j, d, local=False):
        xx = (x + d) % NX
        src = prod.at[i - 1, half, slots(xx)]
        dst = ret.at[j, slots(x)]
        if local:
            return pltpu.make_async_copy(src, dst, ret_recv.at[j, x])
        return pltpu.make_async_remote_copy(
            src_ref=src,
            dst_ref=dst,
            send_sem=ret_send.at[i - 1, half, d],
            recv_sem=ret_recv.at[j, x],
            device_id=(p, at(z - j, xx)),
            device_id_type=MESH,
        )

    def leg_copy(i, half):
        return pltpu.make_async_remote_copy(
            src_ref=prod.at[i - 1, half],
            dst_ref=relay.at[i - 1 - leg, half],
            send_sem=leg_send.at[i - 1, half],
            recv_sem=leg_recv.at[i - 1, half],
            device_id=(p, at(z + (2 * half - 1) * leg, x)),
            device_id_type=MESH,
        )

    def last_leg_copy(d):
        rows = slots((x + d) % NX)
        return pltpu.make_async_remote_copy(
            src_ref=prod.at[steps - 1, 1, rows],
            dst_ref=relay.at[steps - 1 - leg, d % 2, rows],
            send_sem=last_leg_send.at[d],
            recv_sem=last_leg_recv.at[d],
            device_id=(p, at(z + (2 * (d % 2) - 1) * leg, x)),
            device_id_type=MESH,
        )

    def relay_copy(i, half, d):
        xx = (x + d) % NX
        j = i + half * (nz - 2 * i)
        return pltpu.make_async_remote_copy(
            src_ref=relay.at[i - 1 - leg, half, slots(xx)],
            dst_ref=ret.at[j, slots(x)],
            send_sem=relay_send.at[i - 1, half, d],
            recv_sem=ret_recv.at[j, x],
            device_id=(p, at(z + (2 * half - 1) * (i - leg), xx)),
            device_id_type=MESH,
        )

    def pass_on(i):
        for half in range(2):
            leg_copy(i, half).wait_recv()
            for d in range(NX):
                relay_copy(i, half, d).start()

    def pass_on_last():
        for d in range(NX):
            last_leg_copy(d).wait_recv()
            relay_copy(steps, d % 2, d).start()

    def multiply(i):
        for d in range(NX):
            xx = (x + d) % NX
            pltpu.make_async_copy(
                rows_in.at[i - 1, xx], rows_in.at[i - 1, xx], sel_recv.at[i - 1, xx]
            ).wait()
        count = NX * 2 * MOST
        gates = rows_in[i - 1, :, :, width:].reshape(count, LANES).astype(jnp.float32)
        for n in range(0, hidden, 256):
            out = lax.dot_general(
                rows_in[i - 1, :, :, :width].reshape(count, width),
                w_ref[n : n + 256],
                (((1,), (1,)), ((), ())),
                preferred_element_type=jnp.float32,
            )
            for c in range(0, 256, LANES):
                scaled = (out[:, c : c + LANES] * gates).astype(jnp.bfloat16)
                for xx in range(NX):
                    for half in range(2):
                        first = (xx * 2 + half) * MOST
                        prod[
                            i - 1, half, xx * MOST : (xx + 1) * MOST, n + c : n + c + LANES
                        ] = scaled[first : first + MOST]

    def send_back(i):
        @pl.when(i <= leg)
        def _():
            for half, j in enumerate(pair(i)):
                for d in range(NX):
                    ret_copy(i, half, j, d).start()

        @pl.when(i > leg)
        def _():
            for half in range(2):
                leg_copy(i, half).start()

    def send_back_last():
        for d in range(NX):
            last_leg_copy(d).start()
        for d in range(NX):
            ret_copy(steps, 0, 0, d, local=d == 0).start()

    def step(i, carry):
        for c in range(CHUNKS):
            for way in range(2):
                last = steps - 1 + (c * 2 // CHUNKS == way)

                @pl.when(i <= last)
                def _():
                    ring(way, i, up_ref, c).wait_recv()

                @pl.when(i < last)
                def _():
                    ring(way, i + 1, tok.at[i if way == 0 else nz - i], c).start()

        @pl.when(i < steps)
        def _():
            ring_table(0, i, table.at[0]).wait_recv()

        @pl.when(i < steps - 1)
        def _():
            ring_table(0, i + 1, table.at[i]).start()

        ring_table(1, i, table.at[0]).wait_recv()

        @pl.when(i < steps)
        def _():
            ring_table(1, i + 1, table.at[nz - i]).start()

        @pl.when(i == steps)
        def _():
            own_copy.wait()

        choose(i)

        @pl.when(i > 3)
        def _():
            multiply(i - 3)
            send_back(i - 3)

        @pl.when(i > leg + 4)
        def _():
            pass_on(i - 4)

        return carry

    lax.fori_loop(1, steps + 1, step, 0)
    multiply(steps - 2)
    send_back(steps - 2)
    multiply(steps - 1)
    send_back(steps - 1)
    multiply(steps)
    send_back_last()
    for i in range(max(leg, steps - 4) + 1, steps):
        pass_on(i)
    acc[...] = jnp.zeros_like(acc)

    def place(i, carry):
        a, b = pair(i)
        for j in (a, b):
            for xx in range(NX):
                here = ret.at[j, xx * MOST : (xx + 1) * MOST]
                pltpu.make_async_copy(here, here, ret_recv.at[j, xx]).wait()
        span = NX * MOST
        part = min(128, routes)
        lane_q = iota((part, 2 * span), 1)
        want = jnp.where(lane_q < span, a * span + lane_q, (b - 1) * span + lane_q).astype(
            jnp.float32
        )
        rows = jnp.concatenate([ret[a], ret[b]], axis=0)
        for r in range(0, routes, part):
            pick = (pos[r : r + part, : 2 * span] == want).astype(jnp.bfloat16)
            for n in range(0, hidden, 256):
                acc[r : r + part, n : n + 256] += jnp.dot(
                    pick, rows[:, n : n + 256], preferred_element_type=jnp.float32
                )
        return carry

    lax.fori_loop(1, leg, place, 0)
    pass_on_last()
    lax.fori_loop(leg, steps + 1, place, 0)
    out_ref[...] = acc[...].astype(jnp.bfloat16)

    def drain(i, carry):
        for c in range(CHUNKS):
            for way in range(2):
                last = steps - 1 + (c * 2 // CHUNKS == way)
                pl.when(i <= last)(lambda: ring(way, i, up_ref, c).wait_send())
        pl.when(i < steps)(lambda: ring_table(0, i, table.at[0]).wait_send())
        ring_table(1, i, table.at[0]).wait_send()
        for xx in range(NX):
            sel_copy(i, xx).wait_send()

        @pl.when(i <= leg)
        def _():
            for half, j in enumerate(pair(i)):
                for d in range(NX):
                    ret_copy(i, half, j, d).wait_send()

        @pl.when((i > leg) & (i < steps))
        def _():
            for half in range(2):
                leg_copy(i, half).wait_send()
                for d in range(NX):
                    relay_copy(i, half, d).wait_send()

        return carry

    lax.fori_loop(1, steps + 1, drain, 0)
    for d in range(NX):
        last_leg_copy(d).wait_send()
        relay_copy(steps, d % 2, d).wait_send()
        if d > 0:
            ret_copy(steps, 0, 0, d).wait_send()


def per_device(pipes, experts, upstream, expert_ids, gate_weights, expert_weight):
    _, tokens, width = upstream.shape
    topk = expert_ids.shape[2]
    hidden = expert_weight.shape[2]
    nz = experts // NX
    steps = nz // 2
    routes = tokens * topk
    dma = pltpu.SemaphoreType.DMA
    out = pl.pallas_call(
        functools.partial(kernel, pipes, experts),
        out_shape=jax.ShapeDtypeStruct((routes, hidden), jnp.bfloat16),
        in_specs=[
            pl.BlockSpec(memory_space=pltpu.HBM),
            pl.BlockSpec(memory_space=pltpu.HBM),
            pl.BlockSpec(memory_space=pltpu.HBM),
            pl.BlockSpec(memory_space=pltpu.HBM),
        ],
        out_specs=pl.BlockSpec(memory_space=pltpu.VMEM),
        scratch_shapes=[
            pltpu.VMEM((nz, tokens, width), jnp.bfloat16),
            pltpu.VMEM((nz, MOST, LANES), jnp.bfloat16),
            pltpu.VMEM((MOST, LANES), jnp.bfloat16),
            pltpu.VMEM((steps, NX, 2 * MOST, width + LANES), jnp.bfloat16),
            pltpu.VMEM((steps, NX, 2 * MOST, width + LANES), jnp.bfloat16),
            pltpu.VMEM((steps, 2, NX * MOST, hidden), jnp.bfloat16),
            pltpu.VMEM((steps // 2, 2, NX * MOST, hidden), jnp.bfloat16),
            pltpu.VMEM((nz, NX * MOST, hidden), jnp.bfloat16),
            pltpu.VMEM((routes, hidden), jnp.float32),
            pltpu.VMEM((routes, LANES), jnp.float32),
            pltpu.VMEM((hidden, width), jnp.bfloat16),
            pltpu.VMEM((topk, tokens), jnp.int32),
            pltpu.VMEM((topk, tokens), jnp.bfloat16),
            dma((4,)),
            dma((2, steps + 1, CHUNKS)),
            dma((2, steps + 1, CHUNKS)),
            dma((2, steps + 1)),
            dma((2, steps + 1)),
            dma((2,)),
            dma((steps, NX)),
            dma((steps, NX)),
            dma((steps, 2, NX)),
            dma((nz, NX)),
            dma((steps, 2)),
            dma((steps, 2)),
            dma((NX,)),
            dma((NX,)),
            dma((steps, 2, NX)),
        ],
        compiler_params=pltpu.CompilerParams(
            collective_id=0, has_side_effects=True, vmem_limit_bytes=62 * 1024 * 1024
        ),
        cost_estimate=pl.CostEstimate(
            flops=2 * 2 * routes * width * hidden, bytes_accessed=8 << 20, transcendentals=0
        ),
    )(
        upstream[0],
        jnp.swapaxes(expert_ids[0], 0, 1),
        jnp.swapaxes(gate_weights[0], 0, 1),
        expert_weight[0, 0],
    )
    return out.reshape(1, tokens, topk, hidden)


def solution(mesh):
    in_specs = (
        P("pipe", "expert", None),
        P("pipe", "expert", None),
        P("pipe", "expert", None),
        P("pipe", "expert", None, None),
    )
    out_specs = P("pipe", "expert", None, None)
    return jax.shard_map(
        functools.partial(per_device, mesh.shape["pipe"], mesh.shape["expert"]),
        mesh=mesh,
        in_specs=in_specs,
        out_specs=out_specs,
        check_vma=False,
    )
```

```python
import functools

import jax
import jax.numpy as jnp
from jax import lax
from jax.experimental import pallas as pl
from jax.experimental.pallas import tpu as pltpu
from jax.sharding import PartitionSpec as P

MESH = pl.DeviceIdType.MESH
NX = 4
MOST = 16
LANES = 128
HALF = 64
CHUNKS = 2


def iota(shape, dim):
    return lax.broadcasted_iota(jnp.int32, shape, dim)


def kernel(
    pipes,
    experts,
    up_ref,
    ids_hbm,
    gates_ref,
    w_hbm,
    out_ref,
    tok,
    table,
    own_table,
    sel,
    rows_in,
    prod,
    relay,
    ret,
    acc,
    pos,
    w_ref,
    ids_ref,
    local_sem,
    ring_send,
    ring_recv,
    table_send,
    table_recv,
    shift_sem,
    sel_send,
    sel_recv,
    ret_send,
    ret_recv,
    leg_recv,
    last_leg_recv,
    relay_send,
):
    nz = experts // NX
    steps = nz // 2
    tokens, width = up_ref.shape
    topk = ids_hbm.shape[0]
    hidden = w_hbm.shape[0]
    p = lax.axis_index("pipe")
    e = lax.axis_index("expert")
    z = e // NX
    x = e % NX
    after = (p + 1) % pipes
    before = (p + pipes - 1) % pipes

    leg = steps // 2

    def at(zz, xx):
        return ((zz + nz) % nz) * NX + xx

    def await_all(ref, sem):
        pltpu.make_async_copy(ref, ref, sem).wait()

    def slots(xx):
        return pl.ds(pl.multiple_of(xx * MOST, MOST), MOST)

    barrier = pltpu.get_barrier_semaphore()

    for other in (at(z + 1, x), at(z - 1, x)):
        pl.semaphore_signal(barrier, inc=1, device_id=(p, other), device_id_type=MESH)
    for xx in range(NX):
        pl.semaphore_signal(barrier, inc=1, device_id=(after, at(z, xx)), device_id_type=MESH)
    pl.semaphore_signal(barrier, inc=1, device_id=(before, e), device_id_type=MESH)
    ids_copy = pltpu.make_async_copy(ids_hbm, ids_ref, local_sem.at[2])
    ids_copy.start()
    own_copy = pltpu.make_async_copy(up_ref, tok.at[0], local_sem.at[0])
    own_copy.start()
    w_copy = pltpu.make_async_copy(w_hbm, w_ref, local_sem.at[1])
    w_copy.start()
    pl.semaphore_wait(barrier, 2 + NX + 1)

    def ring(direction, hop, src, c):
        dst = hop if direction == 0 else nz - hop
        part = pl.ds(c * (tokens // CHUNKS), tokens // CHUNKS)
        return pltpu.make_async_remote_copy(
            src_ref=src.at[part],
            dst_ref=tok.at[dst, part],
            send_sem=ring_send.at[0],
            recv_sem=ring_recv.at[direction, hop - 1, c],
            device_id=(p, at(z + 1 - 2 * direction, x)),
            device_id_type=MESH,
        )

    def ring_table(direction, hop, src):
        dst = hop if direction == 0 else nz - hop
        return pltpu.make_async_remote_copy(
            src_ref=src,
            dst_ref=table.at[dst],
            send_sem=table_send.at[0],
            recv_sem=table_recv.at[direction, hop - 1],
            device_id=(p, at(z + 1 - 2 * direction, x)),
            device_id_type=MESH,
        )

    for c in range(CHUNKS):
        for way in range(2):
            ring(way, 1, up_ref, c).start()
    ids_copy.wait()

    packed = jnp.concatenate(
        [ids_ref[...].astype(jnp.float32), gates_ref[...].astype(jnp.float32)], axis=0
    ).astype(jnp.bfloat16)
    eye = (iota((tokens, tokens), 0) == iota((tokens, tokens), 1)).astype(jnp.bfloat16)
    columns = lax.dot_general(
        eye, packed, (((1,), (1,)), ((), ())), preferred_element_type=jnp.float32
    )
    lane = iota((tokens, LANES), 1)
    lane_expert = (lane % HALF).astype(jnp.float32)
    named = jnp.zeros((tokens, LANES), jnp.float32)
    gate = jnp.zeros((tokens, LANES), jnp.float32)
    for k in range(topk):
        hit = columns[:, k : k + 1] == lane_expert
        named = jnp.where(hit, 1.0, named)
        gate = jnp.where(hit, columns[:, topk + k : topk + k + 1], gate)
    lower = (iota((tokens, tokens), 1) < iota((tokens, tokens), 0)).astype(jnp.bfloat16)
    rank = jnp.dot(lower, named.astype(jnp.bfloat16), preferred_element_type=jnp.float32)
    value = jnp.where(lane < HALF, (iota((tokens, LANES), 0) + 1).astype(jnp.float32), gate)
    value = jnp.where(named > 0.5, value, 0.0)
    table_rows = [
        jnp.sum(jnp.where(rank == float(r), value, 0.0), axis=0, keepdims=True)
        for r in range(MOST)
    ]
    own_table[...] = jnp.concatenate(table_rows, axis=0).astype(jnp.bfloat16)

    shift = pltpu.make_async_remote_copy(
        src_ref=own_table,
        dst_ref=table.at[0],
        send_sem=shift_sem.at[0],
        recv_sem=shift_sem.at[1],
        device_id=(after, e),
        device_id_type=MESH,
    )
    shift.start()

    ranks = []
    for k in range(topk):
        hit = (columns[:, k : k + 1] == lane_expert) & (lane < HALF)
        ranks.append(jnp.sum(jnp.where(hit, rank, 0.0), axis=1, keepdims=True))
    lane8 = iota((tokens, 2 * topk), 1)
    both = jnp.where(lane8 < topk, columns, 0.0)
    for k in range(topk):
        both = jnp.where(lane8 == topk + k, ranks[k], both)
    routes = tokens * topk
    spread = (iota((routes, tokens), 0) // topk == iota((routes, tokens), 1)).astype(jnp.bfloat16)
    by_route = jnp.dot(spread, both.astype(jnp.bfloat16), preferred_element_type=jnp.float32)
    which = iota((routes, 2 * topk), 0) % topk
    lane_r = iota((routes, 2 * topk), 1)
    slot = jnp.sum(
        jnp.where(lane_r == which, by_route * MOST, 0.0)
        + jnp.where(lane_r == which + topk, by_route, 0.0),
        axis=1,
        keepdims=True,
    )
    slot = slot - (z * (NX * MOST)).astype(jnp.float32)
    slot = jnp.where(slot < 0.0, slot + float(experts * MOST), slot)
    pos[...] = jnp.broadcast_to(slot, (routes, LANES))

    shift.wait()
    ring_table(0, 1, table.at[0]).start()
    ring_table(1, 1, table.at[0]).start()
    w_copy.wait()

    def pair(i):
        return i % steps, nz - i

    def sel_copy(i, xx):
        return pltpu.make_async_remote_copy(
            src_ref=sel.at[i - 1, xx],
            dst_ref=rows_in.at[i - 1, x],
            send_sem=sel_send.at[0],
            recv_sem=sel_recv.at[i - 1],
            device_id=(before, at(z, xx)),
            device_id_type=MESH,
        )

    def choose(i):
        table_lane = iota((MOST, LANES), 1)
        token_lane = (iota((MOST, tokens), 1) + 1).astype(jnp.float32)
        for half, j in enumerate(pair(i)):
            slots = table[j].astype(jnp.float32)
            picks = []
            for xx in range(NX):
                expert = at(z, xx)
                token = jnp.sum(
                    jnp.where(table_lane == expert, slots, 0.0), axis=1, keepdims=True
                )
                weight = jnp.sum(
                    jnp.where(table_lane == expert + HALF, slots, 0.0), axis=1, keepdims=True
                )
                picks.append((token == token_lane).astype(jnp.bfloat16))
                sel[i - 1, xx, half * MOST : (half + 1) * MOST, width:] = jnp.broadcast_to(
                    weight, (MOST, LANES)
                ).astype(jnp.bfloat16)
            pick = jnp.concatenate(picks, axis=0)
            part = min(512, width)
            for c in range(0, width, part):
                rows = jnp.dot(
                    pick, tok[j, :, c : c + part], preferred_element_type=jnp.float32
                ).astype(jnp.bfloat16)
                for xx in range(NX):
                    sel[i - 1, xx, half * MOST : (half + 1) * MOST, c : c + part] = rows[
                        xx * MOST : (xx + 1) * MOST
                    ]
        for d in range(NX):
            sel_copy(i, (x + d) % NX).start()

    def ret_copy(i, half, j, d, last=False, local=False):
        xx = (x + d) % NX
        src = prod.at[i - 1, half, slots(xx)]
        dst = ret.at[j, slots(x)]
        if local:
            return pltpu.make_async_copy(src, dst, ret_recv.at[j])
        return pltpu.make_async_remote_copy(
            src_ref=src,
            dst_ref=dst,
            send_sem=ret_send.at[1 if last else 0],
            recv_sem=ret_recv.at[j],
            device_id=(p, at(z - j, xx)),
            device_id_type=MESH,
        )

    def leg_copy(i, half):
        return pltpu.make_async_remote_copy(
            src_ref=prod.at[i - 1, half],
            dst_ref=relay.at[i - 1 - leg, half],
            send_sem=ret_send.at[0],
            recv_sem=leg_recv.at[i - 1 - leg, half],
            device_id=(p, at(z + (2 * half - 1) * leg, x)),
            device_id_type=MESH,
        )

    def last_leg_copy(d):
        rows = slots((x + d) % NX)
        return pltpu.make_async_remote_copy(
            src_ref=prod.at[steps - 1, 1, rows],
            dst_ref=relay.at[steps - 1 - leg, d % 2, rows],
            send_sem=ret_send.at[2],
            recv_sem=last_leg_recv.at[d],
            device_id=(p, at(z + (2 * (d % 2) - 1) * leg, x)),
            device_id_type=MESH,
        )

    def relay_copy(i, half, d, last=False):
        xx = (x + d) % NX
        j = i + half * (nz - 2 * i)
        return pltpu.make_async_remote_copy(
            src_ref=relay.at[i - 1 - leg, half, slots(xx)],
            dst_ref=ret.at[j, slots(x)],
            send_sem=relay_send.at[1 if last else 0],
            recv_sem=ret_recv.at[j],
            device_id=(p, at(z + (2 * half - 1) * (i - leg), xx)),
            device_id_type=MESH,
        )

    def pass_on(i):
        for half in range(2):
            leg_copy(i, half).wait_recv()
            for d in range(NX):
                relay_copy(i, half, d).start()

    def pass_on_last():
        for d in range(NX):
            last_leg_copy(d).wait_recv()
            relay_copy(steps, d % 2, d, last=True).start()

    def multiply(i):
        await_all(rows_in.at[i - 1], sel_recv.at[i - 1])
        count = NX * 2 * MOST
        gates = rows_in[i - 1, :, :, width:].reshape(count, LANES).astype(jnp.float32)
        for n in range(0, hidden, 256):
            out = lax.dot_general(
                rows_in[i - 1, :, :, :width].reshape(count, width),
                w_ref[n : n + 256],
                (((1,), (1,)), ((), ())),
                preferred_element_type=jnp.float32,
            )
            for c in range(0, 256, LANES):
                scaled = (out[:, c : c + LANES] * gates).astype(jnp.bfloat16)
                for xx in range(NX):
                    for half in range(2):
                        first = (xx * 2 + half) * MOST
                        prod[
                            i - 1, half, xx * MOST : (xx + 1) * MOST, n + c : n + c + LANES
                        ] = scaled[first : first + MOST]

    def send_back(i):
        @pl.when(i <= leg)
        def _():
            for half, j in enumerate(pair(i)):
                for d in range(NX):
                    ret_copy(i, half, j, d).start()

        @pl.when(i > leg)
        def _():
            for half in range(2):
                leg_copy(i, half).start()

    def send_back_last():
        for d in range(NX):
            last_leg_copy(d).start()
        for d in range(NX):
            ret_copy(steps, 0, 0, d, last=True, local=d == 0).start()

    def step(i, carry):
        for c in range(CHUNKS):
            for way in range(2):
                last = steps - 1 + (c * 2 // CHUNKS == way)

                @pl.when(i <= last)
                def _():
                    ring(way, i, up_ref, c).wait_recv()

                @pl.when(i < last)
                def _():
                    ring(way, i + 1, tok.at[i if way == 0 else nz - i], c).start()

        @pl.when(i < steps)
        def _():
            ring_table(0, i, table.at[0]).wait_recv()

        @pl.when(i < steps - 1)
        def _():
            ring_table(0, i + 1, table.at[i]).start()

        ring_table(1, i, table.at[0]).wait_recv()

        @pl.when(i < steps)
        def _():
            ring_table(1, i + 1, table.at[nz - i]).start()

        @pl.when(i == steps)
        def _():
            own_copy.wait()

        choose(i)

        @pl.when(i > 3)
        def _():
            multiply(i - 3)
            send_back(i - 3)

        return carry

    lax.fori_loop(1, steps + 1, step, 0)
    for i in (steps - 2, steps - 1):
        multiply(i)
        send_back(i)
    multiply(steps)
    send_back_last()
    for i in range(leg + 1, steps):
        pass_on(i)
    acc[...] = jnp.zeros_like(acc)

    def place(i, carry):
        a, b = pair(i)
        for j in (a, b):
            await_all(ret.at[j], ret_recv.at[j])
        span = NX * MOST
        part = min(128, routes)
        lane_q = iota((part, 2 * span), 1)
        want = jnp.where(lane_q < span, a * span + lane_q, (b - 1) * span + lane_q).astype(
            jnp.float32
        )
        rows = jnp.concatenate([ret[a], ret[b]], axis=0)
        for r in range(0, routes, part):
            pick = (pos[r : r + part, : 2 * span] == want).astype(jnp.bfloat16)
            for n in range(0, hidden, 256):
                acc[r : r + part, n : n + 256] += jnp.dot(
                    pick, rows[:, n : n + 256], preferred_element_type=jnp.float32
                )
        return carry

    lax.fori_loop(1, leg, place, 0)
    pass_on_last()

    await_all(tok.at[pl.ds(0, nz - 1)], ring_send.at[0])
    await_all(table.at[pl.ds(0, nz - 1)], table_send.at[0])
    await_all(sel, sel_send.at[0])
    await_all(prod.at[pl.ds(0, steps - 1)], ret_send.at[0])
    await_all(prod.at[steps - 1, 0, pl.ds(0, (NX - 1) * MOST)], ret_send.at[1])
    await_all(prod.at[steps - 1, 1], ret_send.at[2])
    if steps - 1 > leg:
        await_all(relay.at[pl.ds(0, steps - 1 - leg)], relay_send.at[0])
    await_all(relay.at[steps - 1 - leg, 0], relay_send.at[1])

    lax.fori_loop(leg, steps + 1, place, 0)
    out_ref[...] = acc[...].astype(jnp.bfloat16)


def per_device(pipes, experts, upstream, expert_ids, gate_weights, expert_weight):
    _, tokens, width = upstream.shape
    topk = expert_ids.shape[2]
    hidden = expert_weight.shape[2]
    nz = experts // NX
    steps = nz // 2
    routes = tokens * topk
    dma = pltpu.SemaphoreType.DMA
    out = pl.pallas_call(
        functools.partial(kernel, pipes, experts),
        out_shape=jax.ShapeDtypeStruct((routes, hidden), jnp.bfloat16),
        in_specs=[
            pl.BlockSpec(memory_space=pltpu.HBM),
            pl.BlockSpec(memory_space=pltpu.HBM),
            pl.BlockSpec(memory_space=pltpu.VMEM),
            pl.BlockSpec(memory_space=pltpu.HBM),
        ],
        out_specs=pl.BlockSpec(memory_space=pltpu.VMEM),
        scratch_shapes=[
            pltpu.VMEM((nz, tokens, width), jnp.bfloat16),
            pltpu.VMEM((nz, MOST, LANES), jnp.bfloat16),
            pltpu.VMEM((MOST, LANES), jnp.bfloat16),
            pltpu.VMEM((steps, NX, 2 * MOST, width + LANES), jnp.bfloat16),
            pltpu.VMEM((steps, NX, 2 * MOST, width + LANES), jnp.bfloat16),
            pltpu.VMEM((steps, 2, NX * MOST, hidden), jnp.bfloat16),
            pltpu.VMEM((steps // 2, 2, NX * MOST, hidden), jnp.bfloat16),
            pltpu.VMEM((nz, NX * MOST, hidden), jnp.bfloat16),
            pltpu.VMEM((routes, hidden), jnp.float32),
            pltpu.VMEM((routes, LANES), jnp.float32),
            pltpu.VMEM((hidden, width), jnp.bfloat16),
            pltpu.VMEM((topk, tokens), jnp.int32),
            dma((3,)),
            dma((1,)),
            dma((2, steps, CHUNKS)),
            dma((1,)),
            dma((2, steps)),
            dma((2,)),
            dma((1,)),
            dma((steps,)),
            dma((3,)),
            dma((nz,)),
            dma((max(1, steps - 1 - steps // 2), 2)),
            dma((NX,)),
            dma((2,)),
        ],
        compiler_params=pltpu.CompilerParams(
            collective_id=0, has_side_effects=True, vmem_limit_bytes=44 * 1024 * 1024
        ),
        cost_estimate=pl.CostEstimate(
            flops=2 * 2 * routes * width * hidden, bytes_accessed=8 << 20, transcendentals=0
        ),
    )(
        pltpu.with_memory_space_constraint(upstream[0], pltpu.HBM),
        pltpu.with_memory_space_constraint(jnp.swapaxes(expert_ids[0], 0, 1), pltpu.HBM),
        jnp.swapaxes(gate_weights[0], 0, 1),
        pltpu.with_memory_space_constraint(expert_weight[0, 0], pltpu.HBM),
    )
    return out.reshape(1, tokens, topk, hidden)


def solution(mesh):
    in_specs = (
        P("pipe", "expert", None),
        P("pipe", "expert", None),
        P("pipe", "expert", None),
        P("pipe", "expert", None, None),
    )
    out_specs = P("pipe", "expert", None, None)
    return jax.shard_map(
        functools.partial(per_device, mesh.shape["pipe"], mesh.shape["expert"]),
        mesh=mesh,
        in_specs=in_specs,
        out_specs=out_specs,
        check_vma=False,
    )
```

```python
import functools

import jax
import jax.numpy as jnp
from jax import lax
from jax.experimental import pallas as pl
from jax.experimental.pallas import tpu as pltpu
from jax.sharding import PartitionSpec as P

MESH = pl.DeviceIdType.MESH
NX = 4
MOST = 16
LANES = 128
HALF = 64
CHUNKS = 2


def iota(shape, dim):
    return lax.broadcasted_iota(jnp.int32, shape, dim)


def kernel(
    pipes,
    experts,
    up_ref,
    ids_hbm,
    gates_ref,
    w_hbm,
    out_ref,
    tok,
    table,
    own_table,
    sel,
    rows_in,
    prod,
    relay,
    ret,
    acc,
    pos,
    w_ref,
    ids_ref,
    local_sem,
    ring_send,
    ring_recv,
    table_send,
    table_recv,
    shift_sem,
    sel_send,
    sel_recv,
    ret_send,
    ret_recv,
    leg_recv,
    last_leg_recv,
    relay_send,
):
    nz = experts // NX
    steps = nz // 2
    tokens, width = up_ref.shape
    topk = ids_hbm.shape[0]
    hidden = w_hbm.shape[0]
    p = lax.axis_index("pipe")
    e = lax.axis_index("expert")
    z = e // NX
    x = e % NX
    after = (p + 1) % pipes
    before = (p + pipes - 1) % pipes

    leg = steps // 2

    def at(zz, xx):
        return ((zz + nz) % nz) * NX + xx

    def await_all(ref, sem):
        pltpu.make_async_copy(ref, ref, sem).wait()

    def slots(xx):
        return pl.ds(pl.multiple_of(xx * MOST, MOST), MOST)

    barrier = pltpu.get_barrier_semaphore()

    for other in (at(z + 1, x), at(z - 1, x)):
        pl.semaphore_signal(barrier, inc=1, device_id=(p, other), device_id_type=MESH)
    for xx in range(NX):
        pl.semaphore_signal(barrier, inc=1, device_id=(after, at(z, xx)), device_id_type=MESH)
    pl.semaphore_signal(barrier, inc=1, device_id=(before, e), device_id_type=MESH)
    ids_copy = pltpu.make_async_copy(ids_hbm, ids_ref, local_sem.at[2])
    ids_copy.start()
    own_copy = pltpu.make_async_copy(up_ref, tok.at[0], local_sem.at[0])
    own_copy.start()
    w_copy = pltpu.make_async_copy(w_hbm, w_ref, local_sem.at[1])
    w_copy.start()
    pl.semaphore_wait(barrier, 2 + NX + 1)

    def ring(direction, hop, src, c):
        dst = hop if direction == 0 else nz - hop
        part = pl.ds(c * (tokens // CHUNKS), tokens // CHUNKS)
        return pltpu.make_async_remote_copy(
            src_ref=src.at[part],
            dst_ref=tok.at[dst, part],
            send_sem=ring_send.at[0],
            recv_sem=ring_recv.at[direction, hop - 1, c],
            device_id=(p, at(z + 1 - 2 * direction, x)),
            device_id_type=MESH,
        )

    def ring_table(direction, hop, src):
        dst = hop if direction == 0 else nz - hop
        return pltpu.make_async_remote_copy(
            src_ref=src,
            dst_ref=table.at[dst],
            send_sem=table_send.at[0],
            recv_sem=table_recv.at[direction, hop - 1],
            device_id=(p, at(z + 1 - 2 * direction, x)),
            device_id_type=MESH,
        )

    for c in range(CHUNKS):
        for way in range(2):
            ring(way, 1, up_ref, c).start()
    ids_copy.wait()

    packed = jnp.concatenate(
        [ids_ref[...].astype(jnp.float32), gates_ref[...].astype(jnp.float32)], axis=0
    ).astype(jnp.bfloat16)
    eye = (iota((tokens, tokens), 0) == iota((tokens, tokens), 1)).astype(jnp.bfloat16)
    columns = lax.dot_general(
        eye, packed, (((1,), (1,)), ((), ())), preferred_element_type=jnp.float32
    )
    lane = iota((tokens, LANES), 1)
    lane_expert = (lane % HALF).astype(jnp.float32)
    named = jnp.zeros((tokens, LANES), jnp.float32)
    gate = jnp.zeros((tokens, LANES), jnp.float32)
    for k in range(topk):
        hit = columns[:, k : k + 1] == lane_expert
        named = jnp.where(hit, 1.0, named)
        gate = jnp.where(hit, columns[:, topk + k : topk + k + 1], gate)
    lower = (iota((tokens, tokens), 1) < iota((tokens, tokens), 0)).astype(jnp.bfloat16)
    rank = jnp.dot(lower, named.astype(jnp.bfloat16), preferred_element_type=jnp.float32)
    value = jnp.where(lane < HALF, (iota((tokens, LANES), 0) + 1).astype(jnp.float32), gate)
    value = jnp.where(named > 0.5, value, 0.0)
    table_rows = [
        jnp.sum(jnp.where(rank == float(r), value, 0.0), axis=0, keepdims=True)
        for r in range(MOST)
    ]
    own_table[...] = jnp.concatenate(table_rows, axis=0).astype(jnp.bfloat16)

    shift = pltpu.make_async_remote_copy(
        src_ref=own_table,
        dst_ref=table.at[0],
        send_sem=shift_sem.at[0],
        recv_sem=shift_sem.at[1],
        device_id=(after, e),
        device_id_type=MESH,
    )
    shift.start()

    shift.wait()
    ring_table(0, 1, table.at[0]).start()
    ring_table(1, 1, table.at[0]).start()
    w_copy.wait()

    def pair(i):
        return i % steps, nz - i

    def sel_copy(i, xx):
        return pltpu.make_async_remote_copy(
            src_ref=sel.at[i - 1, xx],
            dst_ref=rows_in.at[i - 1, x],
            send_sem=sel_send.at[0],
            recv_sem=sel_recv.at[i - 1],
            device_id=(before, at(z, xx)),
            device_id_type=MESH,
        )

    def pick_rows(i, half, j):
        table_lane = iota((MOST, LANES), 1)
        token_lane = (iota((MOST, tokens), 1) + 1).astype(jnp.float32)
        slots = table[j].astype(jnp.float32)
        picks = []
        for xx in range(NX):
            expert = at(z, xx)
            token = jnp.sum(
                jnp.where(table_lane == expert, slots, 0.0), axis=1, keepdims=True
            )
            weight = jnp.sum(
                jnp.where(table_lane == expert + HALF, slots, 0.0), axis=1, keepdims=True
            )
            picks.append((token == token_lane).astype(jnp.bfloat16))
            sel[i - 1, xx, half * MOST : (half + 1) * MOST, width:] = jnp.broadcast_to(
                weight, (MOST, LANES)
            ).astype(jnp.bfloat16)
        pick = jnp.concatenate(picks, axis=0)
        part = min(512, width)
        for c in range(0, width, part):
            rows = jnp.dot(
                pick, tok[j, :, c : c + part], preferred_element_type=jnp.float32
            ).astype(jnp.bfloat16)
            for xx in range(NX):
                sel[i - 1, xx, half * MOST : (half + 1) * MOST, c : c + part] = rows[
                    xx * MOST : (xx + 1) * MOST
                ]

    def choose(i):
        own, other = pair(i)
        pl.when(i < steps)(lambda: pick_rows(i, 0, own))
        pick_rows(i, 1, other)
        for d in range(NX):
            sel_copy(i, (x + d) % NX).start()

    def ret_copy(i, half, j, d, last=False, local=False):
        xx = (x + d) % NX
        src = prod.at[i - 1, half, slots(xx)]
        dst = ret.at[j, slots(x)]
        if local:
            return pltpu.make_async_copy(src, dst, ret_recv.at[j])
        return pltpu.make_async_remote_copy(
            src_ref=src,
            dst_ref=dst,
            send_sem=ret_send.at[1 if last else 0],
            recv_sem=ret_recv.at[j],
            device_id=(p, at(z - j, xx)),
            device_id_type=MESH,
        )

    def leg_copy(i, half):
        return pltpu.make_async_remote_copy(
            src_ref=prod.at[i - 1, half],
            dst_ref=relay.at[i - 1 - leg, half],
            send_sem=ret_send.at[0],
            recv_sem=leg_recv.at[i - 1 - leg, half],
            device_id=(p, at(z + (2 * half - 1) * leg, x)),
            device_id_type=MESH,
        )

    def last_leg_copy(d):
        rows = slots((x + d) % NX)
        return pltpu.make_async_remote_copy(
            src_ref=prod.at[steps - 1, 1, rows],
            dst_ref=relay.at[steps - 1 - leg, d % 2, rows],
            send_sem=ret_send.at[2],
            recv_sem=last_leg_recv.at[d],
            device_id=(p, at(z + (2 * (d % 2) - 1) * leg, x)),
            device_id_type=MESH,
        )

    def relay_copy(i, half, d, last=False):
        xx = (x + d) % NX
        j = i + half * (nz - 2 * i)
        return pltpu.make_async_remote_copy(
            src_ref=relay.at[i - 1 - leg, half, slots(xx)],
            dst_ref=ret.at[j, slots(x)],
            send_sem=relay_send.at[1 if last else 0],
            recv_sem=ret_recv.at[j],
            device_id=(p, at(z + (2 * half - 1) * (i - leg), xx)),
            device_id_type=MESH,
        )

    def pass_on(i):
        for half in range(2):
            leg_copy(i, half).wait_recv()
            for d in range(NX):
                relay_copy(i, half, d).start()

    def pass_on_last():
        for d in range(NX):
            last_leg_copy(d).wait_recv()
            relay_copy(steps, d % 2, d, last=True).start()

    def multiply(i):
        await_all(rows_in.at[i - 1], sel_recv.at[i - 1])
        count = NX * 2 * MOST
        gates = rows_in[i - 1, :, :, width:].reshape(count, LANES).astype(jnp.float32)
        for n in range(0, hidden, 256):
            out = lax.dot_general(
                rows_in[i - 1, :, :, :width].reshape(count, width),
                w_ref[n : n + 256],
                (((1,), (1,)), ((), ())),
                preferred_element_type=jnp.float32,
            )
            for c in range(0, 256, LANES):
                scaled = (out[:, c : c + LANES] * gates).astype(jnp.bfloat16)
                for xx in range(NX):
                    for half in range(2):
                        first = (xx * 2 + half) * MOST
                        prod[
                            i - 1, half, xx * MOST : (xx + 1) * MOST, n + c : n + c + LANES
                        ] = scaled[first : first + MOST]

    def send_back(i):
        @pl.when(i <= leg)
        def _():
            for half, j in enumerate(pair(i)):
                for d in range(NX):
                    ret_copy(i, half, j, d).start()

        @pl.when(i > leg)
        def _():
            for half in range(2):
                leg_copy(i, half).start()

    def send_back_last():
        for d in range(NX):
            last_leg_copy(d).start()
        for d in range(NX):
            ret_copy(steps, 0, 0, d, last=True, local=d == 0).start()

    own_copy.wait()
    pick_rows(steps, 0, 0)

    def step(i, carry):
        for c in range(CHUNKS):
            for way in range(2):
                last = steps - 1 + (c * 2 // CHUNKS == way)

                @pl.when(i <= last)
                def _():
                    ring(way, i, up_ref, c).wait_recv()

                @pl.when(i < last)
                def _():
                    ring(way, i + 1, tok.at[i if way == 0 else nz - i], c).start()

        @pl.when(i < steps)
        def _():
            ring_table(0, i, table.at[0]).wait_recv()

        @pl.when(i < steps - 1)
        def _():
            ring_table(0, i + 1, table.at[i]).start()

        ring_table(1, i, table.at[0]).wait_recv()

        @pl.when(i < steps)
        def _():
            ring_table(1, i + 1, table.at[nz - i]).start()

        choose(i)

        @pl.when(i > 3)
        def _():
            multiply(i - 3)
            send_back(i - 3)

        return carry

    lax.fori_loop(1, steps + 1, step, 0)
    for i in (steps - 2, steps - 1):
        multiply(i)
        send_back(i)
    multiply(steps)
    send_back_last()
    for i in range(leg + 1, steps):
        pass_on(i)
    ranks = []
    for k in range(topk):
        hit = (columns[:, k : k + 1] == lane_expert) & (lane < HALF)
        ranks.append(jnp.sum(jnp.where(hit, rank, 0.0), axis=1, keepdims=True))
    lane8 = iota((tokens, 2 * topk), 1)
    both = jnp.where(lane8 < topk, columns, 0.0)
    for k in range(topk):
        both = jnp.where(lane8 == topk + k, ranks[k], both)
    routes = tokens * topk
    spread = (iota((routes, tokens), 0) // topk == iota((routes, tokens), 1)).astype(jnp.bfloat16)
    by_route = jnp.dot(spread, both.astype(jnp.bfloat16), preferred_element_type=jnp.float32)
    which = iota((routes, 2 * topk), 0) % topk
    lane_r = iota((routes, 2 * topk), 1)
    slot = jnp.sum(
        jnp.where(lane_r == which, by_route * MOST, 0.0)
        + jnp.where(lane_r == which + topk, by_route, 0.0),
        axis=1,
        keepdims=True,
    )
    slot = slot - (z * (NX * MOST)).astype(jnp.float32)
    slot = jnp.where(slot < 0.0, slot + float(experts * MOST), slot)
    pos[...] = jnp.broadcast_to(slot, (routes, LANES))

    acc[...] = jnp.zeros_like(acc)

    def place(i, carry, last=False):
        a, b = pair(i)
        for j in (a, b):
            await_all(ret.at[j], ret_recv.at[j])
        span = NX * MOST
        part = min(128, routes)
        lane_q = iota((part, 2 * span), 1)
        want = jnp.where(lane_q < span, a * span + lane_q, (b - 1) * span + lane_q).astype(
            jnp.float32
        )
        rows = jnp.concatenate([ret[a], ret[b]], axis=0)
        for r in range(0, routes, part):
            pick = (pos[r : r + part, : 2 * span] == want).astype(jnp.bfloat16)
            for n in range(0, hidden, 256):
                more = acc[r : r + part, n : n + 256] + jnp.dot(
                    pick, rows[:, n : n + 256], preferred_element_type=jnp.float32
                )
                if last:
                    out_ref[r : r + part, n : n + 256] = more.astype(jnp.bfloat16)
                else:
                    acc[r : r + part, n : n + 256] = more
        return carry

    lax.fori_loop(1, leg, place, 0)
    pass_on_last()

    await_all(tok.at[pl.ds(0, nz - 1)], ring_send.at[0])
    await_all(table.at[pl.ds(0, nz - 1)], table_send.at[0])
    await_all(sel, sel_send.at[0])
    await_all(prod.at[pl.ds(0, steps - 1)], ret_send.at[0])
    await_all(prod.at[steps - 1, 0, pl.ds(0, (NX - 1) * MOST)], ret_send.at[1])
    await_all(prod.at[steps - 1, 1], ret_send.at[2])
    if steps - 1 > leg:
        await_all(relay.at[pl.ds(0, steps - 1 - leg)], relay_send.at[0])
    await_all(relay.at[steps - 1 - leg, 0], relay_send.at[1])

    lax.fori_loop(leg, steps, place, 0)
    place(steps, 0, last=True)


def per_device(pipes, experts, upstream, expert_ids, gate_weights, expert_weight):
    _, tokens, width = upstream.shape
    topk = expert_ids.shape[2]
    hidden = expert_weight.shape[2]
    nz = experts // NX
    steps = nz // 2
    routes = tokens * topk
    dma = pltpu.SemaphoreType.DMA
    out = pl.pallas_call(
        functools.partial(kernel, pipes, experts),
        out_shape=jax.ShapeDtypeStruct((routes, hidden), jnp.bfloat16),
        in_specs=[
            pl.BlockSpec(memory_space=pltpu.HBM),
            pl.BlockSpec(memory_space=pltpu.HBM),
            pl.BlockSpec(memory_space=pltpu.VMEM),
            pl.BlockSpec(memory_space=pltpu.HBM),
        ],
        out_specs=pl.BlockSpec(memory_space=pltpu.VMEM),
        scratch_shapes=[
            pltpu.VMEM((nz, tokens, width), jnp.bfloat16),
            pltpu.VMEM((nz, MOST, LANES), jnp.bfloat16),
            pltpu.VMEM((MOST, LANES), jnp.bfloat16),
            pltpu.VMEM((steps, NX, 2 * MOST, width + LANES), jnp.bfloat16),
            pltpu.VMEM((steps, NX, 2 * MOST, width + LANES), jnp.bfloat16),
            pltpu.VMEM((steps, 2, NX * MOST, hidden), jnp.bfloat16),
            pltpu.VMEM((steps // 2, 2, NX * MOST, hidden), jnp.bfloat16),
            pltpu.VMEM((nz, NX * MOST, hidden), jnp.bfloat16),
            pltpu.VMEM((routes, hidden), jnp.float32),
            pltpu.VMEM((routes, LANES), jnp.float32),
            pltpu.VMEM((hidden, width), jnp.bfloat16),
            pltpu.VMEM((topk, tokens), jnp.int32),
            dma((3,)),
            dma((1,)),
            dma((2, steps, CHUNKS)),
            dma((1,)),
            dma((2, steps)),
            dma((2,)),
            dma((1,)),
            dma((steps,)),
            dma((3,)),
            dma((nz,)),
            dma((max(1, steps - 1 - steps // 2), 2)),
            dma((NX,)),
            dma((2,)),
        ],
        compiler_params=pltpu.CompilerParams(
            collective_id=0, has_side_effects=True, vmem_limit_bytes=44 * 1024 * 1024
        ),
        cost_estimate=pl.CostEstimate(
            flops=2 * 2 * routes * width * hidden, bytes_accessed=8 << 20, transcendentals=0
        ),
    )(
        pltpu.with_memory_space_constraint(upstream[0], pltpu.HBM),
        pltpu.with_memory_space_constraint(jnp.swapaxes(expert_ids[0], 0, 1), pltpu.HBM),
        jnp.swapaxes(gate_weights[0], 0, 1),
        pltpu.with_memory_space_constraint(expert_weight[0, 0], pltpu.HBM),
    )
    return out.reshape(1, tokens, topk, hidden)


def solution(mesh):
    in_specs = (
        P("pipe", "expert", None),
        P("pipe", "expert", None),
        P("pipe", "expert", None),
        P("pipe", "expert", None, None),
    )
    out_specs = P("pipe", "expert", None, None)
    return jax.shard_map(
        functools.partial(per_device, mesh.shape["pipe"], mesh.shape["expert"]),
        mesh=mesh,
        in_specs=in_specs,
        out_specs=out_specs,
        check_vma=False,
    )
```
